256 devices in a mesh: dp: 4 (over y_hi, core), row: 16 (over y_lo, z), col: 4 (over x).
Axes of the slice: x: 4, y: 4 (y_hi: 2, y_lo: 2; y = y_hi * 2 + y_lo), z: 8, core: 2. Of those that a mesh axis runs over, the one named last changes fastest.
Arguments:
- tokens: bfloat16 [1024, 8192], P(('dp', 'row'), 'col'), may hold values from -1.5 to 1.5
- w_gate: bfloat16 [8192, 26624], P(('col', 'dp'), 'row'), may hold values from -0.25 to 0.25
- w_up: bfloat16 [8192, 26624], P(('col', 'dp'), 'row'), may hold values from -0.25 to 0.25
- grad_hidden: bfloat16 [1024, 26624], P(('dp', 'col'), 'row'), may hold values from -6 to 6
Outputs:
- hidden: bfloat16 [1024, 26624], P(('dp', 'col'), 'row')
- grad_tokens: bfloat16 [1024, 8192], P(('dp', 'row'), 'col')
- grad_wgate: float32 [8192, 26624], P(('col', 'dp'), 'row')
- grad_wup: float32 [8192, 26624], P(('col', 'dp'), 'row')
The draws below stay inside these ranges and needn't reach their ends.
All inputs are finite; a program needn't handle non-finite values.
Results may differ from the reference program's by a relative error of at most 0.011.
Values may be sent and summed in bfloat16 or wider, within the bound.
No kernel may reach another device: no remote copies, remote signals or barrier semaphores. Data moves between devices by JAX's collectives and lax.ppermute only.
A program may use at most 128 MiB of HBM per device.

```python
import jax
import jax.numpy as jnp
from jax import lax

D = 8192
FF = 26624
TOK_REP = 256
TOKENS = 1024
N_DP = 4


def levels(rng, shape, split, least, largest):
    factor_of = 1.0
    for position, parts in split:
        draws = jax.random.uniform(jax.random.fold_in(jax.random.fold_in(rng, 6), position), (parts,), jnp.float32, least / len(split), largest / len(split))
        factor_of = factor_of * jnp.repeat(jnp.exp(draws), shape[position] // parts).reshape((-1,) + (1,) * (len(shape) - 1 - position))
    return factor_of


def scatter_about(rng, shape, scale, reach, pieces=(), dtype=jnp.bfloat16):
    array = scale * jax.random.normal(rng, shape, jnp.float32)
    if pieces:
        array = array * levels(rng, shape, pieces, -0.22, 0.18)
    return jnp.clip(array, -reach, reach).astype(dtype)


def setup_inputs(seed: int = 0) -> dict:
    streams_of = jax.random.split(jax.random.key(seed), 5)
    return {
        "tokens": scatter_about(streams_of[0], (TOKENS, D), 0.25, 1.5, ((0, 64), (1, 4))),
        "w_gate": scatter_about(streams_of[1], (D, FF), (D // 16) ** -0.5, 0.25, ((0, 16), (1, 16))),
        "w_up": scatter_about(streams_of[2], (D, FF), (D // 16) ** -0.5, 0.25, ((0, 16), (1, 16))),
        "grad_hidden": scatter_about(streams_of[3], (TOKENS, FF), 1.0, 6.0, ((0, 16), (1, 16))),
    }


def reference(tokens, w_gate, w_up, grad_hidden):
    gate_pre = jnp.dot(tokens, w_gate, preferred_element_type=jnp.float32)
    up_pre = jnp.dot(tokens, w_up, preferred_element_type=jnp.float32)
    logistic = jax.nn.sigmoid(gate_pre)
    hidden = (gate_pre * logistic * up_pre).astype(jnp.bfloat16)
    upstream = grad_hidden.astype(jnp.float32)
    grad_up = (upstream * gate_pre * logistic).astype(jnp.bfloat16)
    grad_gate = (upstream * up_pre * logistic * (1.0 + gate_pre * (1.0 - logistic))).astype(jnp.bfloat16)
    grad_tokens = (jnp.dot(grad_gate, w_gate.T, preferred_element_type=jnp.float32)
                   + jnp.dot(grad_up, w_up.T, preferred_element_type=jnp.float32)).astype(jnp.bfloat16)
    grad_wgate = jnp.zeros((D, FF), jnp.float32)
    grad_wup = jnp.zeros((D, FF), jnp.float32)
    for replica in range(N_DP):
        first = replica * TOK_REP
        chosen = tokens[first:first + TOK_REP].T
        part_gate = jnp.dot(chosen, grad_gate[first:first + TOK_REP], preferred_element_type=jnp.float32)
        part_gate = lax.optimization_barrier(part_gate.astype(jnp.bfloat16))
        grad_wgate = grad_wgate + part_gate.astype(jnp.float32)
        part_up = jnp.dot(chosen, grad_up[first:first + TOK_REP], preferred_element_type=jnp.float32)
        part_up = lax.optimization_barrier(part_up.astype(jnp.bfloat16))
        grad_wup = grad_wup + part_up.astype(jnp.float32)
    return hidden, grad_tokens, grad_wgate, grad_wup
```

```python
import jax
import jax.numpy as jnp
from jax import lax
from jax.sharding import PartitionSpec as P

AXES = ("dp", "row", "col")
CHUNKS = 1


def permutation(move):
    pairs = []
    for dp in range(4):
        for row in range(16):
            for col in range(4):
                x, y_hi, y_lo, z, core = move(col, dp // 2, row // 8, row % 8, dp % 2)
                target = ((y_hi * 2 + core) * 16 + y_lo * 8 + z % 8) * 4 + x
                pairs.append(((dp * 16 + row) * 4 + col, target))
    return pairs


def send(array, x=0, y_hi=0, y_lo=0, z=0, core=0):
    return lax.ppermute(
        array,
        AXES,
        permutation(lambda a, b, c, d, e: (a ^ x, b ^ y_hi, c ^ y_lo, d + z, e ^ core)),
    )


def dot(left, right, contract):
    return lax.dot_general(
        left, right, ((contract[:1], contract[1:]), ((), ())), preferred_element_type=jnp.float32
    )


def wide(array):
    return array.astype(jnp.float32)


def narrow(array):
    return array.astype(jnp.bfloat16)


Z_ORDER = (4, 3, -3, 2, -2, 1, -1)


def on_device(tokens, w_gate, w_up, grad_hidden):
    feats, width = w_gate.shape
    x = lax.axis_index("col")
    y_hi, core = lax.axis_index("dp") // 2, lax.axis_index("dp") % 2
    y_lo, z = lax.axis_index("row") // 8, lax.axis_index("row") % 8
    rows = tokens.shape[0]
    part = rows // CHUNKS
    block = 4 * part

    gate_w = jnp.concatenate([w_gate, send(w_gate, core=1)], axis=0)
    up_w = jnp.concatenate([w_up, send(w_up, core=1)], axis=0)

    count = 32 * part
    src = lax.iota(jnp.int32, count)
    inner = src % part
    d_hi = (src // part) % 2
    d_lo = (src // (2 * part)) % 2
    step = src // (4 * part)
    from_z = (z - step + 8) % 8
    d_x = x ^ ((y_lo ^ d_lo) * 2 + from_z // 4)
    dest = ((d_hi * 4 + d_x) * 4 + from_z % 4) * part + inner
    order = narrow(lax.broadcasted_iota(jnp.int32, (count, count), 0) == dest[None, :])

    quarters = [
        lax.dynamic_slice_in_dim(tokens, ((y_hi ^ (i // 2)) * 2 + (core ^ (i % 2))) * feats, feats, axis=1)
        for i in range(4)
    ]
    near = jnp.concatenate(quarters[:2], axis=1)
    far = jnp.concatenate(quarters[2:], axis=1)

    def gather_tokens(c):
        mine, other = near[c * part : (c + 1) * part], far[c * part : (c + 1) * part]
        piece = jnp.stack(
            [
                jnp.stack([mine, send(other, y_hi=1)]),
                jnp.stack([send(mine, y_lo=1), send(other, y_hi=1, y_lo=1)]),
            ]
        )
        got = {k: send(piece, z=k) for k in Z_ORDER}
        got[0] = piece
        flat = jnp.stack([got[k if k < 5 else k - 8] for k in range(8)]).reshape(count, 2 * feats)
        return narrow(dot(order, flat, (1, 0)))

    def project(tok):
        half = count // 2
        gate_far = narrow(dot(tok[half:], gate_w, (1, 0)))
        got = send(gate_far, y_hi=1)
        up = narrow(dot(tok, up_w, (1, 0))).reshape(2, 4, block, width)
        ups = [send(up[:, k], x=k) for k in (2, 1, 3)]
        gate_near = dot(tok[:half], gate_w, (1, 0))
        gate = narrow(gate_near + wide(got)).reshape(4, block, width)
        gates = [send(gate[k], x=k) for k in (2, 1, 3)]
        up = narrow(wide(up[:, 0]) + wide(ups[0]) + wide(ups[1]) + wide(ups[2]))
        up_far = send(up[1], y_hi=1)
        gate_pre = wide(gate[0]) + wide(gates[0]) + wide(gates[1]) + wide(gates[2])
        return gate_pre, wide(up[0]) + wide(up_far)

    def activate(gate_pre, up_pre, upstream):
        logistic = jax.nn.sigmoid(gate_pre)
        upstream = wide(upstream)
        hidden = narrow(gate_pre * logistic * up_pre)
        grad_up = narrow(upstream * gate_pre * logistic)
        grad_gate = narrow(upstream * up_pre * logistic * (1.0 + gate_pre * (1.0 - logistic)))
        return hidden, grad_gate, grad_up

    def gather_grads(grad_gate, grad_up):
        pair = jnp.stack([grad_up, send(grad_up, y_hi=1)])
        gates = [send(grad_gate, x=k) for k in (2, 1, 3)]
        gates = jnp.concatenate([grad_gate, gates[1], gates[0], gates[2]])
        ups = [send(pair, x=k) for k in (2, 1, 3)]
        gate_all = jnp.concatenate([gates, send(gates, y_hi=1)])
        up_all = jnp.stack([pair, ups[1], ups[0], ups[2]], axis=1).reshape(count, width)
        return gate_all, up_all

    def sum_tokens(gate_all, up_all):
        partial = narrow(dot(gate_all, gate_w, (1, 1)) + dot(up_all, up_w, (1, 1)))
        flat = narrow(dot(order, partial, (0, 0))).reshape(8, 2, 2, part, 2 * feats)
        got = [send(flat[k % 8], z=-k) for k in Z_ORDER]
        total = narrow(sum((wide(g) for g in got), wide(flat[0])))
        from_lo = send(total[1, 0], y_lo=1)
        from_hi = send(total[0, 1], y_hi=1)
        from_both = send(total[1, 1], y_lo=1, y_hi=1)
        mine = narrow(wide(total[0, 0]) + wide(from_lo))
        other = narrow(wide(from_hi) + wide(from_both))
        quarters = [mine[:, :feats], mine[:, feats:], other[:, :feats], other[:, feats:]]
        ordered = []
        for i in range(4):
            a, b = (y_hi == i // 2), (core == i % 2)
            ordered.append(
                jnp.where(
                    a,
                    jnp.where(b, quarters[0], quarters[1]),
                    jnp.where(b, quarters[2], quarters[3]),
                )
            )
        return jnp.concatenate(ordered, axis=1)

    upstream = grad_hidden.reshape(4, CHUNKS, part, width)
    hiddens, tokgrads, toks, gates, ups = [], [], [], [], []
    for c in range(CHUNKS):
        tok = gather_tokens(c)
        gate_pre, up_pre = project(tok)
        hidden, grad_gate, grad_up = activate(gate_pre, up_pre, upstream[:, c].reshape(block, width))
        gate_all, up_all = gather_grads(grad_gate, grad_up)
        tokgrads.append(sum_tokens(gate_all, up_all))
        hiddens.append(hidden.reshape(4, part, width))
        toks += [tok[:, :feats], send(tok[:, feats:], core=1)]
        gates += [gate_all, send(gate_all, core=1)]
        ups += [up_all, send(up_all, core=1)]
    hidden = jnp.stack(hiddens, axis=1).reshape(4 * rows, width)
    grad_tokens = jnp.concatenate(tokgrads, axis=0)
    grad_wgate = sum(dot(t, g, (0, 0)) for t, g in zip(toks, gates))
    grad_wup = sum(dot(t, g, (0, 0)) for t, g in zip(toks, ups))
    return (hidden, grad_tokens, grad_wgate, grad_wup)


def solution(mesh):
    placed = (
        P(("dp", "row"), "col"),
        P(("col", "dp"), "row"),
        P(("col", "dp"), "row"),
        P(("dp", "col"), "row"),
    )
    return jax.shard_map(
        on_device,
        mesh=mesh,
        in_specs=placed,
        out_specs=(
            P(("dp", "col"), "row"),
            P(("dp", "row"), "col"),
            P(("col", "dp"), "row"),
            P(("col", "dp"), "row"),
        ),
        check_vma=False,
    )
```

```python
import jax
import jax.numpy as jnp
from jax import lax
from jax.experimental import pallas as pl
from jax.experimental.pallas import tpu as pltpu
from jax.sharding import PartitionSpec as P

AXES = ("dp", "row", "col")
MEBI = 1 << 20


def permutation(move):
    pairs = []
    for dp in range(4):
        for row in range(16):
            for col in range(4):
                x, y_hi, y_lo, z, core = move(col, dp // 2, row // 8, row % 8, dp % 2)
                target = ((y_hi * 2 + core) * 16 + y_lo * 8 + z % 8) * 4 + x
                pairs.append(((dp * 16 + row) * 4 + col, target))
    return pairs


def send(array, x=0, y_hi=0, y_lo=0, z=0, core=0):
    return lax.ppermute(
        array,
        AXES,
        permutation(lambda a, b, c, d, e: (a ^ x, b ^ y_hi, c ^ y_lo, d + z, e ^ core)),
    )


def dot(left, right, contract):
    return lax.dot_general(
        left, right, ((contract[:1], contract[1:]), ((), ())), preferred_element_type=jnp.float32
    )


def wide(array):
    return array.astype(jnp.float32)


def narrow(array):
    return array.astype(jnp.bfloat16)


def whole(shape):
    return pl.BlockSpec(shape, lambda i: (0,) * len(shape))


def dot_rows(left, right):
    return dot(left, right, (1, 1))


SMALL = pl.CostEstimate(flops=1 << 20, bytes_accessed=1 << 20, transcendentals=0)


def call(kernel, grid, in_specs, out_specs, out_shape, limit, scratch=()):
    return pl.pallas_call(
        kernel,
        grid=(grid,),
        in_specs=in_specs,
        out_specs=out_specs,
        out_shape=out_shape,
        scratch_shapes=list(scratch),
        compiler_params=pltpu.CompilerParams(vmem_limit_bytes=limit * MEBI),
        cost_estimate=SMALL,
    )


def columns(width):
    return [slice(at, min(width, at + 256)) for at in range(0, width, 256)]


def product(tok, first, second, span):
    feats = first.shape[0]
    return dot(tok[:, :feats], first[:, span], (1, 0)) + dot(tok[:, feats:], second[:, span], (1, 0))


def gate_far_kernel(tok, first, second, out):
    for span in columns(first.shape[1]):
        out[:, span] = narrow(product(tok, first, second, span))


def gate_near_kernel(tok, first, second, far, *outs):
    rows = outs[0].shape[0]
    for span in columns(first.shape[1]):
        total = narrow(product(tok, first, second, span) + wide(far[:, span]))
        for n, out in enumerate(outs):
            out[:, span] = total[n * rows : (n + 1) * rows]


def up_kernel(tok, first, second, *outs):
    rows = outs[0].shape[1]
    for span in columns(first.shape[1]):
        total = narrow(product(tok, first, second, span))
        for n, out in enumerate(outs):
            out[0, :, span] = total[n * rows : (n + 1) * rows]


def gate_far(tok, weights):
    count, feats = tok.shape
    shape = weights[0].shape
    half = pl.BlockSpec((count // 2, feats), lambda i: (1, 0))
    out = (count // 2, shape[1])
    return call(
        gate_far_kernel,
        1,
        [half, whole(shape), whole(shape)],
        whole(out),
        jax.ShapeDtypeStruct(out, jnp.bfloat16),
        24,
    )(tok, *weights)


def gate_near(tok, weights, far):
    count, feats = tok.shape
    shape = weights[0].shape
    half = pl.BlockSpec((count // 2, feats), lambda i: (0, 0))
    out = (count // 8, shape[1])
    return call(
        gate_near_kernel,
        1,
        [half, whole(shape), whole(shape), whole(far.shape)],
        [whole(out)] * 4,
        [jax.ShapeDtypeStruct(out, jnp.bfloat16)] * 4,
        24,
    )(tok, *weights, far)


def up_blocks(tok, weights):
    count, feats = tok.shape
    shape = weights[0].shape
    half = pl.BlockSpec((count // 2, feats), lambda i: (i, 0))
    out = (2, count // 8, shape[1])
    return call(
        up_kernel,
        2,
        [half, whole(shape), whole(shape)],
        [pl.BlockSpec((1,) + out[1:], lambda i: (i, 0, 0))] * 4,
        [jax.ShapeDtypeStruct(out, jnp.bfloat16)] * 4,
        24,
    )(tok, *weights)


def token_grad_kernel(gates, far_gates, ups, undo, wg0, wg1, wu0, wu1, *rest):
    outs, held = rest[:-1], rest[-1]
    rows = gates.shape[0]

    def tile(wg, wu):
        for half, gate in enumerate((gates, far_gates)):
            span = slice(half * rows, (half + 1) * rows)
            held[span, :] = narrow(dot_rows(gate[...], wg[...]) + dot_rows(ups[span, :], wu[...]))

    mine = pl.program_id(0) == 0

    @pl.when(mine)
    def _():
        tile(wg0, wu0)

    @pl.when(jnp.logical_not(mine))
    def _():
        tile(wg1, wu1)

    placed = narrow(dot(undo[...], held[...], (1, 0)))
    size = outs[0].shape[0]
    for n, out in enumerate(outs):
        out[...] = placed[n * size : (n + 1) * size]


def token_grads(gates, far_gates, ups, undo, gate_w, up_w):
    rows, width = gates.shape
    feats = gate_w[0].shape[0]
    out = jax.ShapeDtypeStruct((rows // 2, 2 * feats), jnp.bfloat16)
    return call(
        token_grad_kernel,
        2,
        [whole(gates.shape), whole(gates.shape), whole(ups.shape), whole(undo.shape)]
        + [whole((feats, width))] * 4,
        [pl.BlockSpec((rows // 2, feats), lambda i: (0, i))] * 4,
        [out] * 4,
        36,
        [pltpu.VMEM((2 * rows, feats), jnp.bfloat16)],
    )(gates, far_gates, ups, undo, *gate_w, *up_w)


def weight_grad_kernel(*refs):
    own, other, *grads, out = refs
    rows = grads[0].shape[0]
    for span in columns(out.shape[1]):
        total = None
        for n, grad in enumerate(grads):
            source = own if n < len(grads) // 2 else other
            at = (n % (len(grads) // 2)) * rows
            term = dot(source[:, at : at + rows], grad[:, span], (1, 0))
            total = term if total is None else total + term
        out[:, span] = total


def weight_grad(own, other, grads):
    feats, count = own.shape
    width = grads[0].shape[1]
    side = pl.BlockSpec((feats // 2, count), lambda i: (i, 0))
    return call(
        weight_grad_kernel,
        2,
        [side, side] + [whole(g.shape) for g in grads],
        pl.BlockSpec((feats // 2, width), lambda i: (i, 0)),
        jax.ShapeDtypeStruct((feats, width), jnp.float32),
        24,
    )(own, other, *grads)


def on_device(tokens, w_gate, w_up, grad_hidden):
    feats, width = w_gate.shape
    x = lax.axis_index("col")
    y_hi, core = lax.axis_index("dp") // 2, lax.axis_index("dp") % 2
    y_lo, z = lax.axis_index("row") // 8, lax.axis_index("row") % 8
    rows = tokens.shape[0]
    part = rows
    block = 4 * part

    gate_w = (w_gate, send(w_gate, core=1))
    up_w = (w_up, send(w_up, core=1))

    count = 32 * part
    src = lax.iota(jnp.int32, count)

    def places(d_lo, d_hi, step):
        from_z = (z - step + 8) % 8
        d_x = x ^ ((y_lo ^ d_lo) * 2 + from_z // 4)
        return ((d_hi * 4 + d_x) * 4 + from_z % 4) * part + src % part

    dest = places(src // (16 * part), (src // part) % 2, (src // (2 * part)) % 8)
    order = narrow(lax.broadcasted_iota(jnp.int32, (count, count), 0) == dest[None, :])
    order_turned = narrow(lax.broadcasted_iota(jnp.int32, (count, count), 1) == dest[:, None])
    back = places(src // (16 * part), (src // (8 * part)) % 2, (src // part) % 8)
    undo = narrow(lax.broadcasted_iota(jnp.int32, (count, count), 1) == back[:, None])

    quarters = [
        lax.dynamic_slice_in_dim(tokens, ((y_hi ^ (i // 2)) * 2 + (core ^ (i % 2))) * feats, feats, axis=1)
        for i in range(4)
    ]
    near = jnp.concatenate(quarters[:2], axis=1)
    far = jnp.concatenate(quarters[2:], axis=1)

    def gather_tokens(mine, other):
        piece = jnp.stack([mine, send(other, y_hi=1)])
        piece4 = jnp.stack([send(mine, z=4), send(other, y_hi=1, z=4)])
        pair = jnp.stack([piece, piece4])
        one, seven = send(pair, z=1), send(pair, z=-1)
        two, six = send(piece, z=2), send(piece, z=-2)
        line = jnp.stack([piece, one[0], two, seven[1], piece4, one[1], six, seven[0]])
        flat = jnp.stack([line, send(line, y_lo=1)]).reshape(count, 2 * feats)
        return narrow(dot(order, flat, (1, 0))), narrow(dot(flat, order_turned, (0, 0)))

    def project(tok):
        got = send(gate_far(tok, gate_w), y_hi=1)
        blocks = up_blocks(tok, up_w)
        ups = [send(blocks[k], x=k) for k in (1, 2, 3)]
        up = narrow(sum((wide(u) for u in ups), wide(blocks[0])))
        up_far = send(up[1], y_hi=1)
        gate = gate_near(tok, gate_w, got)
        gates = [send(gate[k], x=k) for k in (1, 2, 3)]
        gate_pre = sum((wide(g) for g in gates), wide(gate[0]))
        return gate_pre, wide(up[0]) + wide(up_far)

    def activate(gate_pre, up_pre, upstream):
        logistic = jax.nn.sigmoid(gate_pre)
        upstream = wide(upstream)
        hidden = narrow(gate_pre * logistic * up_pre)
        grad_up = narrow(upstream * gate_pre * logistic)
        grad_gate = narrow(upstream * up_pre * logistic * (1.0 + gate_pre * (1.0 - logistic)))
        return hidden, grad_gate, grad_up

    def gather_grads(grad_gate, grad_up):
        pair = jnp.stack([grad_up, send(grad_up, y_hi=1)])
        gates = [send(grad_gate, x=k) for k in (2, 1, 3)]
        gates = jnp.concatenate([grad_gate, gates[1], gates[0], gates[2]])
        ups = [send(pair, x=k) for k in (2, 1, 3)]
        far_gates = send(gates, y_hi=1)
        up_all = jnp.stack([pair, ups[1], ups[0], ups[2]], axis=1).reshape(count, width)
        return gates, far_gates, up_all

    def sum_tokens(parts, beside):
        got = [send(parts[1], y_hi=1), send(parts[2], y_lo=1), send(parts[3], y_hi=1, y_lo=1)]
        got, beside = lax.optimization_barrier((got, beside))
        shape = (8, part, 2 * feats)
        line = narrow(
            jnp.stack(
                [
                    (wide(parts[0]) + wide(got[1])).reshape(shape),
                    (wide(got[0]) + wide(got[2])).reshape(shape),
                ],
                axis=1,
            )
        )
        one, seven = send(jnp.stack([line[1], line[5]]), z=-1), send(jnp.stack([line[7], line[3]]), z=1)
        two, six = send(line[2], z=-2), send(line[6], z=2)
        here = wide(line[0]) + wide(one[0]) + wide(seven[0]) + wide(two) + wide(six)
        there = narrow(wide(line[4]) + wide(one[1]) + wide(seven[1]))
        mine, other = narrow(here + wide(send(there, z=4)))
        quarters = [mine[:, :feats], mine[:, feats:], other[:, :feats], other[:, feats:]]
        ordered = []
        for i in range(4):
            a, b = (y_hi == i // 2), (core == i % 2)
            ordered.append(
                jnp.where(
                    a,
                    jnp.where(b, quarters[0], quarters[1]),
                    jnp.where(b, quarters[2], quarters[3]),
                )
            )
        return jnp.concatenate(ordered, axis=1), *beside

    tok, turned = gather_tokens(near, far)
    gate_pre, up_pre = project(tok)
    hidden, grad_gate, grad_up = activate(gate_pre, up_pre, grad_hidden)
    gates, far_gates, ups = gather_grads(grad_gate, grad_up)
    own_turned, other_turned = turned[:feats], send(turned[feats:], core=1)
    gates_too, far_too, ups_too = send(gates, core=1), send(far_gates, core=1), send(ups, core=1)
    parts = token_grads(gates, far_gates, ups, undo, gate_w, up_w)
    grad_wgate = weight_grad(own_turned, other_turned, [gates, far_gates, gates_too, far_too])
    grad_wup = weight_grad(own_turned, other_turned, [ups, ups_too])
    grad_tokens, grad_wgate, grad_wup = sum_tokens(parts, (grad_wgate, grad_wup))
    return (hidden, grad_tokens, grad_wgate, grad_wup)


def solution(mesh):
    placed = (
        P(("dp", "row"), "col"),
        P(("col", "dp"), "row"),
        P(("col", "dp"), "row"),
        P(("dp", "col"), "row"),
    )
    return jax.shard_map(
        on_device,
        mesh=mesh,
        in_specs=placed,
        out_specs=(
            P(("dp", "col"), "row"),
            P(("dp", "row"), "col"),
            P(("col", "dp"), "row"),
            P(("col", "dp"), "row"),
        ),
        check_vma=False,
    )
```

```python
import functools

import jax
import jax.numpy as jnp
from jax import lax
from jax.experimental import pallas as pl
from jax.experimental.pallas import tpu as pltpu
from jax.sharding import PartitionSpec as P

AXES = ("dp", "row", "col")
MEBI = 1 << 20


def permutation(move):
    pairs = []
    for dp in range(4):
        for row in range(16):
            for col in range(4):
                x, y_hi, y_lo, z, core = move(col, dp // 2, row // 8, row % 8, dp % 2)
                target = ((y_hi * 2 + core) * 16 + y_lo * 8 + z % 8) * 4 + x
                pairs.append(((dp * 16 + row) * 4 + col, target))
    return pairs


def send(array, x=0, y_hi=0, y_lo=0, z=0, core=0):
    return lax.ppermute(
        array,
        AXES,
        permutation(lambda a, b, c, d, e: (a ^ x, b ^ y_hi, c ^ y_lo, d + z, e ^ core)),
    )


def dot(left, right, contract):
    return lax.dot_general(
        left, right, ((contract[:1], contract[1:]), ((), ())), preferred_element_type=jnp.float32
    )


def wide(array):
    return array.astype(jnp.float32)


def narrow(array):
    return array.astype(jnp.bfloat16)


def whole(shape):
    return pl.BlockSpec(memory_space=pltpu.VMEM)


def dot_rows(left, right):
    return dot(left, right, (1, 1))


SMALL = pl.CostEstimate(flops=1 << 20, bytes_accessed=1 << 20, transcendentals=0)


def call(kernel, grid, in_specs, out_specs, out_shape, limit, scratch=()):
    return pl.pallas_call(
        kernel,
        grid=(grid,),
        in_specs=in_specs,
        out_specs=out_specs,
        out_shape=out_shape,
        scratch_shapes=list(scratch),
        compiler_params=pltpu.CompilerParams(vmem_limit_bytes=limit * MEBI),
        cost_estimate=SMALL,
    )


def columns(width):
    return [slice(at, min(width, at + 256)) for at in range(0, width, 256)]


def product(near, far, first, second, span):
    return dot(near[...], first[:, span], (1, 0)) + dot(far[...], second[:, span], (1, 0))


def gate_far_kernel(near, distant, first, second, out):
    for span in columns(first.shape[1]):
        out[:, span] = narrow(product(near, distant, first, second, span))


def gate_near_kernel(near, distant, first, second, far, *outs):
    rows = outs[0].shape[0]
    for span in columns(first.shape[1]):
        total = narrow(product(near, distant, first, second, span) + wide(far[:, span]))
        for n, out in enumerate(outs):
            out[:, span] = total[n * rows : (n + 1) * rows]


def up_kernel(near, distant, first, second, *outs):
    rows = outs[0].shape[1]
    for span in columns(first.shape[1]):
        total = narrow(product(near, distant, first, second, span))
        for n, out in enumerate(outs):
            out[0, :, span] = total[n * rows : (n + 1) * rows]


def gate_far(tok, weights):
    count, feats = tok[0].shape
    shape = weights[0].shape
    half = pl.BlockSpec((count // 2, feats), lambda i: (1, 0))
    out = (count // 2, shape[1])
    return call(
        gate_far_kernel,
        1,
        [half, half, whole(shape), whole(shape)],
        whole(out),
        jax.ShapeDtypeStruct(out, jnp.bfloat16),
        12,
    )(*tok, *weights)


def gate_near(tok, weights, far):
    count, feats = tok[0].shape
    shape = weights[0].shape
    half = pl.BlockSpec((count // 2, feats), lambda i: (0, 0))
    out = (count // 8, shape[1])
    return call(
        gate_near_kernel,
        1,
        [half, half, whole(shape), whole(shape), whole(far.shape)],
        [whole(out)] * 4,
        [jax.ShapeDtypeStruct(out, jnp.bfloat16)] * 4,
        12,
    )(*tok, *weights, far)


def up_blocks(tok, weights):
    count, feats = tok[0].shape
    shape = weights[0].shape
    half = pl.BlockSpec((count // 2, feats), lambda i: (i, 0))
    out = (2, count // 8, shape[1])
    return call(
        up_kernel,
        2,
        [half, half, whole(shape), whole(shape)],
        [pl.BlockSpec((1,) + out[1:], lambda i: (i, 0, 0))] * 4,
        [jax.ShapeDtypeStruct(out, jnp.bfloat16)] * 4,
        12,
    )(*tok, *weights)


def join_kernel(count, *refs):
    arrays, outs = refs[:count], refs[count:]
    for out in outs:
        at = 0
        for array in arrays:
            rows = array.shape[0]
            if at + rows <= out.shape[0]:
                out[at : at + rows, :] = array[...]
            at += rows


def join(arrays, lengths):
    width = arrays[0].shape[1]
    return call(
        functools.partial(join_kernel, len(arrays)),
        1,
        [whole(a.shape) for a in arrays],
        [whole((n, width)) for n in lengths],
        [jax.ShapeDtypeStruct((n, width), jnp.bfloat16) for n in lengths],
        8,
    )(*arrays)


def place_kernel(first, second, order, *outs):
    half, feats = first.shape[0], first.shape[1] // 2
    for n, out in enumerate(outs):
        span = slice(n * feats, (n + 1) * feats)
        out[...] = narrow(
            dot(order[:, :half], first[:, span], (1, 0))
            + dot(order[:, half:], second[:, span], (1, 0))
        )


def place(first, second, order):
    out = (order.shape[0], first.shape[1] // 2)
    return call(
        place_kernel,
        1,
        [whole(first.shape), whole(second.shape), whole(order.shape)],
        [whole(out)] * 2,
        [jax.ShapeDtypeStruct(out, jnp.bfloat16)] * 2,
        12,
    )(first, second, order)


def token_grad_kernel(gates, far_gates, ups, undo, wg0, wg1, wu0, wu1, *rest):
    outs, held = rest[:-1], rest[-1]
    rows = gates.shape[0]

    def tile(wg, wu):
        for half, gate in enumerate((gates, far_gates)):
            span = slice(half * rows, (half + 1) * rows)
            held[span, :] = narrow(dot_rows(gate[...], wg[...]) + dot_rows(ups[span, :], wu[...]))

    mine = pl.program_id(0) == 0

    @pl.when(mine)
    def _():
        tile(wg0, wu0)

    @pl.when(jnp.logical_not(mine))
    def _():
        tile(wg1, wu1)

    placed = narrow(dot(undo[...], held[...], (1, 0)))
    size = outs[0].shape[0]
    for n, out in enumerate(outs):
        out[...] = placed[n * size : (n + 1) * size]


def token_grads(gates, far_gates, ups, undo, gate_w, up_w):
    rows, width = gates.shape
    feats = gate_w[0].shape[0]
    out = jax.ShapeDtypeStruct((rows // 2, 2 * feats), jnp.bfloat16)
    return call(
        token_grad_kernel,
        2,
        [whole(gates.shape), whole(gates.shape), whole(ups.shape), whole(undo.shape)]
        + [whole((feats, width))] * 4,
        [pl.BlockSpec((rows // 2, feats), lambda i: (0, i))] * 4,
        [out] * 4,
        16,
        [pltpu.VMEM((2 * rows, feats), jnp.bfloat16)],
    )(gates, far_gates, ups, undo, *gate_w, *up_w)


def weight_grad_kernel(*refs):
    own, other, *grads, out = refs
    rows = grads[0].shape[0]
    for span in columns(out.shape[1]):
        total = None
        for n, grad in enumerate(grads):
            source = own if n < len(grads) // 2 else other
            at = (n % (len(grads) // 2)) * rows
            term = dot(source[at : at + rows, :], grad[:, span], (0, 0))
            total = term if total is None else total + term
        out[:, span] = total


def weight_grad(own, other, grads):
    count, feats = own.shape
    width = grads[0].shape[1]
    side = pl.BlockSpec((count, feats // 2), lambda i: (0, i))
    return call(
        weight_grad_kernel,
        2,
        [side, side] + [whole(g.shape) for g in grads],
        pl.BlockSpec((feats // 2, width), lambda i: (i, 0)),
        jax.ShapeDtypeStruct((feats, width), jnp.float32),
        12,
    )(own, other, *grads)


def on_device(tokens, w_gate, w_up, grad_hidden):
    feats, width = w_gate.shape
    x = lax.axis_index("col")
    y_hi, core = lax.axis_index("dp") // 2, lax.axis_index("dp") % 2
    y_lo, z = lax.axis_index("row") // 8, lax.axis_index("row") % 8
    rows = tokens.shape[0]
    part = rows
    block = 4 * part


    gate_w = (w_gate, send(w_gate, core=1))
    up_w = (w_up, send(w_up, core=1))

    count = 32 * part
    src = lax.iota(jnp.int32, count)

    def places(d_lo, d_hi, step):
        from_z = (z - step + 8) % 8
        d_x = x ^ ((y_lo ^ d_lo) * 2 + from_z // 4)
        return ((d_hi * 4 + d_x) * 4 + from_z % 4) * part + src % part

    slot = (src // (2 * part)) % 8
    step = sum(jnp.where(slot == n, k, 0) for n, k in enumerate((0, 4, 1, 5, 7, 3, 2, 6)))
    dest = places(src // (16 * part), (src // part) % 2, step)
    order = narrow(lax.broadcasted_iota(jnp.int32, (count, count), 0) == dest[None, :])
    back = places(src // (16 * part), (src // (8 * part)) % 2, (src // part) % 8)
    undo = narrow(lax.broadcasted_iota(jnp.int32, (count, count), 1) == back[:, None])

    quarters = [
        lax.dynamic_slice_in_dim(tokens, ((y_hi ^ (i // 2)) * 2 + (core ^ (i % 2))) * feats, feats, axis=1)
        for i in range(4)
    ]
    near = jnp.concatenate(quarters[:2], axis=1)
    far = jnp.concatenate(quarters[2:], axis=1)

    def gather_tokens(mine, other):
        pair, piece = join(
            [mine, send(other, y_hi=1), send(mine, z=4), send(other, y_hi=1, z=4)],
            [4 * part, 2 * part],
        )
        one, seven = send(pair, z=1), send(pair, z=-1)
        two, six = send(piece, z=2), send(piece, z=-2)
        (line,) = join([pair, one, seven, two, six], [16 * part])
        return line

    def project(tok, gate_w, up_w):
        first = gate_far(tok, gate_w)
        got = send(first, y_hi=1)
        blocks = up_blocks(tok, up_w)
        ups = [send(blocks[k], x=k) for k in (1, 2, 3)]
        up = narrow(sum((wide(u) for u in ups), wide(blocks[0])))
        up_far = send(up[1], y_hi=1)
        gate = gate_near(tok, gate_w, got)
        gates = [send(gate[k], x=k) for k in (1, 2, 3)]
        gate_pre = sum((wide(g) for g in gates), wide(gate[0]))
        return gate_pre, wide(up[0]) + wide(up_far)

    def activate(gate_pre, up_pre, upstream):
        logistic = jax.nn.sigmoid(gate_pre)
        upstream = wide(upstream)
        hidden = narrow(gate_pre * logistic * up_pre)
        grad_up = narrow(upstream * gate_pre * logistic)
        grad_gate = narrow(upstream * up_pre * logistic * (1.0 + gate_pre * (1.0 - logistic)))
        return hidden, grad_gate, grad_up

    def gather_grads(grad_gate, grad_up):
        pair = jnp.stack([grad_up, send(grad_up, y_hi=1)])
        gates = [send(grad_gate, x=k) for k in (2, 1, 3)]
        gates = jnp.concatenate([grad_gate, gates[1], gates[0], gates[2]])
        ups = [send(pair, x=k) for k in (2, 1, 3)]
        far_gates = send(gates, y_hi=1)
        up_all = jnp.stack([pair, ups[1], ups[0], ups[2]], axis=1).reshape(count, width)
        return gates, far_gates, up_all

    def sum_tokens(parts, beside):
        got = [send(parts[1], y_hi=1), send(parts[2], y_lo=1), send(parts[3], y_hi=1, y_lo=1)]
        got, beside = lax.optimization_barrier((got, beside))
        shape = (8, part, 2 * feats)
        line = narrow(
            jnp.stack(
                [
                    (wide(parts[0]) + wide(got[1])).reshape(shape),
                    (wide(got[0]) + wide(got[2])).reshape(shape),
                ],
                axis=1,
            )
        )
        one, seven = send(jnp.stack([line[1], line[5]]), z=-1), send(jnp.stack([line[7], line[3]]), z=1)
        two, six = send(line[2], z=-2), send(line[6], z=2)
        here = wide(line[0]) + wide(one[0]) + wide(seven[0]) + wide(two) + wide(six)
        there = narrow(wide(line[4]) + wide(one[1]) + wide(seven[1]))
        mine, other = narrow(here + wide(send(there, z=4)))
        quarters = [mine[:, :feats], mine[:, feats:], other[:, :feats], other[:, feats:]]
        ordered = []
        for i in range(4):
            a, b = (y_hi == i // 2), (core == i % 2)
            ordered.append(
                jnp.where(
                    a,
                    jnp.where(b, quarters[0], quarters[1]),
                    jnp.where(b, quarters[2], quarters[3]),
                )
            )
        return jnp.concatenate(ordered, axis=1), *beside

    line = gather_tokens(near, far)
    tok = place(line, send(line, y_lo=1), order)
    gate_pre, up_pre = project(tok, gate_w, up_w)
    hidden, grad_gate, grad_up = activate(gate_pre, up_pre, grad_hidden)
    gates, far_gates, ups = gather_grads(grad_gate, grad_up)
    parts = token_grads(gates, far_gates, ups, undo, gate_w, up_w)
    gates_too, far_too, ups_too = send(gates, core=1), send(far_gates, core=1), send(ups, core=1)
    tok_too = send(tok[1], core=1)
    grad_wgate = weight_grad(tok[0], tok_too, [gates, far_gates, gates_too, far_too])
    grad_wup = weight_grad(tok[0], tok_too, [ups, ups_too])
    grad_tokens, grad_wgate, grad_wup = sum_tokens(parts, (grad_wgate, grad_wup))
    return (hidden, grad_tokens, grad_wgate, grad_wup)


def solution(mesh):
    placed = (
        P(("dp", "row"), "col"),
        P(("col", "dp"), "row"),
        P(("col", "dp"), "row"),
        P(("dp", "col"), "row"),
    )
    return jax.shard_map(
        on_device,
        mesh=mesh,
        in_specs=placed,
        out_specs=(
            P(("dp", "col"), "row"),
            P(("dp", "row"), "col"),
            P(("col", "dp"), "row"),
            P(("col", "dp"), "row"),
        ),
        check_vma=False,
    )
```

```python
import functools

import jax
import jax.numpy as jnp
from jax import lax
from jax.experimental import pallas as pl
from jax.experimental.pallas import tpu as pltpu
from jax.sharding import PartitionSpec as P

AXES = ("dp", "row", "col")
MEBI = 1 << 20


def permutation(move):
    pairs = []
    for dp in range(4):
        for row in range(16):
            for col in range(4):
                x, y_hi, y_lo, z, core = move(col, dp // 2, row // 8, row % 8, dp % 2)
                target = ((y_hi * 2 + core) * 16 + y_lo * 8 + z % 8) * 4 + x
                pairs.append(((dp * 16 + row) * 4 + col, target))
    return pairs


def send(array, x=0, y_hi=0, y_lo=0, z=0, core=0):
    return lax.ppermute(
        array,
        AXES,
        permutation(lambda a, b, c, d, e: (a ^ x, b ^ y_hi, c ^ y_lo, d + z, e ^ core)),
    )


def dot(left, right, contract):
    return lax.dot_general(
        left, right, ((contract[:1], contract[1:]), ((), ())), preferred_element_type=jnp.float32
    )


def wide(array):
    return array.astype(jnp.float32)


def narrow(array):
    return array.astype(jnp.bfloat16)


def whole(shape):
    return pl.BlockSpec(memory_space=pltpu.VMEM)


def dot_rows(left, right):
    return dot(left, right, (1, 1))


SMALL = pl.CostEstimate(flops=1 << 20, bytes_accessed=1 << 23, transcendentals=0)


def call(kernel, grid, in_specs, out_specs, out_shape, limit, scratch=()):
    return pl.pallas_call(
        kernel,
        grid=(grid,),
        in_specs=in_specs,
        out_specs=out_specs,
        out_shape=out_shape,
        scratch_shapes=list(scratch),
        compiler_params=pltpu.CompilerParams(vmem_limit_bytes=limit * MEBI),
        cost_estimate=SMALL,
    )


def columns(width):
    return [slice(at, min(width, at + 256)) for at in range(0, width, 256)]


def product(near, far, first, second, span):
    return dot(near[...], first[:, span], (1, 0)) + dot(far[...], second[:, span], (1, 0))


def gate_far_kernel(near, distant, first, second, out):
    for span in columns(first.shape[1]):
        out[:, span] = narrow(product(near, distant, first, second, span))


def gate_near_kernel(near, distant, first, second, far, *outs):
    rows = outs[0].shape[0]
    for span in columns(first.shape[1]):
        total = narrow(product(near, distant, first, second, span) + wide(far[:, span]))
        for n, out in enumerate(outs):
            out[:, span] = total[n * rows : (n + 1) * rows]


def up_kernel(near, distant, first, second, *outs):
    rows = outs[0].shape[1]
    for span in columns(first.shape[1]):
        total = narrow(product(near, distant, first, second, span))
        for n, out in enumerate(outs):
            out[0, :, span] = total[n * rows : (n + 1) * rows]


def gate_far(tok, weights):
    count, feats = tok[0].shape
    shape = weights[0].shape
    half = pl.BlockSpec((count // 2, feats), lambda i: (1, 0))
    out = (count // 2, shape[1])
    return call(
        gate_far_kernel,
        1,
        [half, half, whole(shape), whole(shape)],
        whole(out),
        jax.ShapeDtypeStruct(out, jnp.bfloat16),
        12,
    )(*tok, *weights)


def gate_near(tok, weights, far):
    count, feats = tok[0].shape
    shape = weights[0].shape
    half = pl.BlockSpec((count // 2, feats), lambda i: (0, 0))
    out = (count // 8, shape[1])
    return call(
        gate_near_kernel,
        1,
        [half, half, whole(shape), whole(shape), whole(far.shape)],
        [whole(out)] * 4,
        [jax.ShapeDtypeStruct(out, jnp.bfloat16)] * 4,
        12,
    )(*tok, *weights, far)


def up_blocks(tok, weights):
    count, feats = tok[0].shape
    shape = weights[0].shape
    half = pl.BlockSpec((count // 2, feats), lambda i: (i, 0))
    out = (2, count // 8, shape[1])
    return call(
        up_kernel,
        2,
        [half, half, whole(shape), whole(shape)],
        [pl.BlockSpec((1,) + out[1:], lambda i: (i, 0, 0))] * 4,
        [jax.ShapeDtypeStruct(out, jnp.bfloat16)] * 4,
        12,
    )(*tok, *weights)


def join_kernel(count, *refs):
    arrays, outs = refs[:count], refs[count:]
    for out in outs:
        at = 0
        for array in arrays:
            rows = array.shape[0]
            if at + rows <= out.shape[0]:
                out[at : at + rows, :] = array[...]
            at += rows


def join(arrays, lengths):
    width = arrays[0].shape[1]
    return call(
        functools.partial(join_kernel, len(arrays)),
        1,
        [whole(a.shape) for a in arrays],
        [whole((n, width)) for n in lengths],
        [jax.ShapeDtypeStruct((n, width), jnp.bfloat16) for n in lengths],
        8,
    )(*arrays)


def place_kernel(first, second, order, *outs):
    half, feats = first.shape[0], first.shape[1] // 2
    for n, out in enumerate(outs):
        span = slice(n * feats, (n + 1) * feats)
        out[...] = narrow(
            dot(order[:, :half], first[:, span], (1, 0))
            + dot(order[:, half:], second[:, span], (1, 0))
        )


def place(first, second, order):
    out = (order.shape[0], first.shape[1] // 2)
    return call(
        place_kernel,
        1,
        [whole(first.shape), whole(second.shape), whole(order.shape)],
        [whole(out)] * 2,
        [jax.ShapeDtypeStruct(out, jnp.bfloat16)] * 2,
        12,
    )(first, second, order)


def token_grad_kernel(gates, far_gates, ups, undo, wg0, wg1, wu0, wu1, *rest):
    outs, held = rest[:-1], rest[-1]
    rows = gates.shape[0]

    def tile(wg, wu):
        for half, gate in enumerate((gates, far_gates)):
            span = slice(half * rows, (half + 1) * rows)
            held[span, :] = narrow(dot_rows(gate[...], wg[...]) + dot_rows(ups[span, :], wu[...]))

    mine = pl.program_id(0) == 0

    @pl.when(mine)
    def _():
        tile(wg0, wu0)

    @pl.when(jnp.logical_not(mine))
    def _():
        tile(wg1, wu1)

    placed = narrow(dot(undo[...], held[...], (1, 0)))
    size = outs[0].shape[0]
    for n, out in enumerate(outs):
        out[...] = placed[n * size : (n + 1) * size]


def token_grads(gates, far_gates, ups, undo, gate_w, up_w):
    rows, width = gates.shape
    feats = gate_w[0].shape[0]
    out = jax.ShapeDtypeStruct((rows // 2, 2 * feats), jnp.bfloat16)
    return call(
        token_grad_kernel,
        2,
        [whole(gates.shape), whole(gates.shape), whole(ups.shape), whole(undo.shape)]
        + [whole((feats, width))] * 4,
        [pl.BlockSpec((rows // 2, feats), lambda i: (0, i))] * 4,
        [out] * 4,
        16,
        [pltpu.VMEM((2 * rows, feats), jnp.bfloat16)],
    )(gates, far_gates, ups, undo, *gate_w, *up_w)


def weight_grad_kernel(*refs):
    own, other, *grads, out = refs
    rows = grads[0].shape[0]
    for span in columns(out.shape[1]):
        total = None
        for n, grad in enumerate(grads):
            source = own if n < len(grads) // 2 else other
            at = (n % (len(grads) // 2)) * rows
            term = dot(source[at : at + rows, :], grad[:, span], (0, 0))
            total = term if total is None else total + term
        out[:, span] = total


def weight_grad(own, other, grads):
    count, feats = own.shape
    width = grads[0].shape[1]
    side = pl.BlockSpec((count, feats // 2), lambda i: (0, i))
    return call(
        weight_grad_kernel,
        2,
        [side, side] + [whole(g.shape) for g in grads],
        pl.BlockSpec((feats // 2, width), lambda i: (i, 0)),
        jax.ShapeDtypeStruct((feats, width), jnp.float32),
        12,
    )(own, other, *grads)


def on_device(tokens, w_gate, w_up, grad_hidden):
    feats, width = w_gate.shape
    x = lax.axis_index("col")
    y_hi, core = lax.axis_index("dp") // 2, lax.axis_index("dp") % 2
    y_lo, z = lax.axis_index("row") // 8, lax.axis_index("row") % 8
    rows = tokens.shape[0]
    part = rows
    block = 4 * part


    gate_w = (w_gate, send(w_gate, core=1))
    up_w = (w_up, send(w_up, core=1))

    count = 32 * part
    src = lax.iota(jnp.int32, count)

    def places(d_lo, d_hi, step):
        from_z = (z - step + 8) % 8
        d_x = x ^ ((y_lo ^ d_lo) * 2 + from_z // 4)
        return ((d_hi * 4 + d_x) * 4 + from_z % 4) * part + src % part

    slot = (src // (2 * part)) % 8
    step = sum(jnp.where(slot == n, k, 0) for n, k in enumerate((0, 4, 1, 5, 7, 3, 2, 6)))
    dest = places(src // (16 * part), (src // part) % 2, step)
    order = narrow(lax.broadcasted_iota(jnp.int32, (count, count), 0) == dest[None, :])
    back = places(src // (16 * part), (src // (8 * part)) % 2, (src // part) % 8)
    undo = narrow(lax.broadcasted_iota(jnp.int32, (count, count), 1) == back[:, None])

    quarters = [
        lax.dynamic_slice_in_dim(tokens, ((y_hi ^ (i // 2)) * 2 + (core ^ (i % 2))) * feats, feats, axis=1)
        for i in range(4)
    ]
    near = jnp.concatenate(quarters[:2], axis=1)
    far = jnp.concatenate(quarters[2:], axis=1)

    def gather_tokens(mine, other):
        pair, piece = join(
            [mine, send(other, y_hi=1), send(mine, z=4), send(other, y_hi=1, z=4)],
            [4 * part, 2 * part],
        )
        one, seven = send(pair, z=1), send(pair, z=-1)
        two, six = send(piece, z=2), send(piece, z=-2)
        (line,) = join([pair, one, seven, two, six], [16 * part])
        return line

    def project(tok, gate_w, up_w):
        first = gate_far(tok, gate_w)
        got = send(first, y_hi=1)
        blocks = up_blocks(tok, up_w)
        ups = [send(blocks[k], x=k) for k in (1, 2, 3)]
        up = narrow(sum((wide(u) for u in ups), wide(blocks[0])))
        up_far = send(up[1], y_hi=1)
        gate = gate_near(tok, gate_w, got)
        gates = [send(gate[k], x=k) for k in (1, 2, 3)]
        gate_pre = sum((wide(g) for g in gates), wide(gate[0]))
        return gate_pre, wide(up[0]) + wide(up_far)

    def activate(gate_pre, up_pre, upstream):
        logistic = jax.nn.sigmoid(gate_pre)
        upstream = wide(upstream)
        hidden = narrow(gate_pre * logistic * up_pre)
        grad_up = narrow(upstream * gate_pre * logistic)
        grad_gate = narrow(upstream * up_pre * logistic * (1.0 + gate_pre * (1.0 - logistic)))
        return hidden, grad_gate, grad_up

    def gather_grads(grad_gate, grad_up):
        pair = jnp.stack([grad_up, send(grad_up, y_hi=1)])
        gates = [send(grad_gate, x=k) for k in (2, 1, 3)]
        gates = jnp.concatenate([grad_gate, gates[1], gates[0], gates[2]])
        ups = [send(pair, x=k) for k in (2, 1, 3)]
        far_gates = send(gates, y_hi=1)
        up_all = jnp.stack([pair, ups[1], ups[0], ups[2]], axis=1).reshape(count, width)
        return gates, far_gates, up_all

    def sum_tokens(parts, beside):
        got = [send(parts[1], y_hi=1), send(parts[2], y_lo=1), send(parts[3], y_hi=1, y_lo=1)]
        got, beside = lax.optimization_barrier((got, beside))
        shape = (8, part, 2 * feats)
        line = narrow(
            jnp.stack(
                [
                    (wide(parts[0]) + wide(got[1])).reshape(shape),
                    (wide(got[0]) + wide(got[2])).reshape(shape),
                ],
                axis=1,
            )
        )
        one, seven = send(jnp.stack([line[1], line[5]]), z=-1), send(jnp.stack([line[7], line[3]]), z=1)
        two, six = send(line[2], z=-2), send(line[6], z=2)
        here = wide(line[0]) + wide(one[0]) + wide(seven[0]) + wide(two) + wide(six)
        there = narrow(wide(line[4]) + wide(one[1]) + wide(seven[1]))
        mine, other = narrow(here + wide(send(there, z=4)))
        quarters = [mine[:, :feats], mine[:, feats:], other[:, :feats], other[:, feats:]]
        ordered = []
        for i in range(4):
            a, b = (y_hi == i // 2), (core == i % 2)
            ordered.append(
                jnp.where(
                    a,
                    jnp.where(b, quarters[0], quarters[1]),
                    jnp.where(b, quarters[2], quarters[3]),
                )
            )
        return jnp.concatenate(ordered, axis=1), *beside

    line = gather_tokens(near, far)
    tok = place(line, send(line, y_lo=1), order)
    gate_pre, up_pre = project(tok, gate_w, up_w)
    hidden, grad_gate, grad_up = activate(gate_pre, up_pre, grad_hidden)
    gates, far_gates, ups = gather_grads(grad_gate, grad_up)
    parts = token_grads(gates, far_gates, ups, undo, gate_w, up_w)
    gates_too, far_too, ups_too = send(gates, core=1), send(far_gates, core=1), send(ups, core=1)
    tok_too = send(tok[1], core=1)
    grad_wgate = weight_grad(tok[0], tok_too, [gates, far_gates, gates_too, far_too])
    grad_wup = weight_grad(tok[0], tok_too, [ups, ups_too])
    grad_tokens, grad_wgate, grad_wup = sum_tokens(parts, (grad_wgate, grad_wup))
    return (hidden, grad_tokens, grad_wgate, grad_wup)


def solution(mesh):
    placed = (
        P(("dp", "row"), "col"),
        P(("col", "dp"), "row"),
        P(("col", "dp"), "row"),
        P(("dp", "col"), "row"),
    )
    return jax.shard_map(
        on_device,
        mesh=mesh,
        in_specs=placed,
        out_specs=(
            P(("dp", "col"), "row"),
            P(("dp", "row"), "col"),
            P(("col", "dp"), "row"),
            P(("col", "dp"), "row"),
        ),
        check_vma=False,
    )
```
